32 devices in a mesh: groups: 2 (over x), tx: 16 (over z, y, core).
Axes of the slice: x: 2, y: 2, z: 4, core: 2. Of those that a mesh axis runs over, the one named last changes fastest.
Arguments:
- features: bfloat16 [384, 64, 128], P(('groups', 'tx')), parts along dimension 0, may hold values from -6 to 6
- nbr_table: int32 [384, 27], P(('groups', 'tx')), parts along dimension 0, may hold values from 0 to 20, as said below
- rim_slots: int32 [32, 8], P(('groups', 'tx')), parts along dimension 0, may hold values from 0 to 12, as said below
- w_first: bfloat16 [3456, 128], P('tx'), may hold values from -0.1875 to 0.1875
- w_second: bfloat16 [3456, 128], P('tx'), may hold values from -0.1875 to 0.1875
- cotangent: bfloat16 [384, 64, 128], P(('groups', 'tx')), parts along dimension 0, may hold values from -0.059814453 to 0.059814453
Outputs:
- out_map: bfloat16 [384, 64, 128], P(('groups', 'tx')), parts along dimension 0
- grad_first: float32 [6912, 128], P(('groups', 'tx')), parts along dimension 0
- grad_second: float32 [6912, 128], P(('groups', 'tx')), parts along dimension 0
The draws below stay inside these ranges and needn't reach their ends.
There are 2 independent parts, one for each index of `groups`. The reference program is written for one: setup_inputs(seed, part) draws one part's arguments, and reference() takes and returns one part's arrays. A program takes and returns all parts, laid end to end along the dimension named above; an argument that names none is the same for every part. Nothing has to cross between parts.
Inputs may be any that keep to these rules, and one draw needn't show every extreme that they name: `nbr_table`: A tile's bricks lie in 3 brick rows of 2 by 2 positions; the map strips of tiles t and t+1 touch at t's last and t+1's first brick row. Entry q of an active slot names the brick at brick offset q: a slot of the same tile (0 to 11), 12+i for entry i of the previous tile's last-row list, 12 + 4+i for entry i of the next tile's first-row list, or 20 where that brick is inactive or outside the map; every entry of an empty slot is 20. Some tiles have all 12 slots active. `rim_slots`: each half lists the active bricks of that brick row in order of position, then 12 up to 4 entries; every tile has at least one active brick in its first and in its last brick row, and some tiles have 4 in both.
All inputs are finite; a program needn't handle non-finite values.
Results may differ from the reference program's by a relative error of at most 0.0049.
Values may be sent and summed in bfloat16 or wider, within the bound.
A program may use at most 64 MiB of HBM per device.

```python
import jax
import jax.numpy as jnp
import numpy as np
from jax import lax

C = 128
KK = 27
BS = 4
RIM = 4
TROWS = 3
VOX = 64
CAP = 12
TILES = 16
BRICKS = 192


def brick_geometry(key):
    base = jax.random.fold_in(key, 29)
    key_band, key_count, key_place, key_slot = jax.random.split(base, 4)
    tile_count = TILES
    row_count = TROWS
    sentinel = CAP + 2 * RIM
    device = jnp.arange(tile_count, dtype=jnp.int32)
    band_start = jax.random.randint(key_band, (), 0, tile_count, dtype=jnp.int32)
    road = jnp.mod(device - band_start, tile_count) < max(1, tile_count // 16)
    row_index = np.arange(row_count)
    edge_row = (row_index == 0) | (row_index == row_count - 1)
    low_count = jnp.asarray(np.where(edge_row, 1, 0).astype(np.int32))
    counts = low_count[None, :] + jax.random.randint(key_count, (tile_count, row_count), 0, 2, dtype=jnp.int32)
    counts = jnp.where(road[:, None], RIM, counts)
    place_keys = jax.random.split(key_place, tile_count * row_count)
    placing = jax.vmap(lambda subkey: jax.random.permutation(subkey, RIM))(place_keys)
    placing = placing.reshape(tile_count, row_count, RIM).astype(jnp.int32)
    ranking = jnp.argsort(placing, axis=-1).astype(jnp.int32)
    active = (ranking < counts[:, :, None]).astype(jnp.int32)
    active_flat = active.reshape(tile_count, row_count * RIM)
    slot_keys = jax.random.split(key_slot, tile_count)
    slot_order = jax.vmap(lambda subkey: jax.random.permutation(subkey, CAP))(slot_keys).astype(jnp.int32)
    order_index = jnp.clip(jnp.cumsum(active_flat, axis=1) - 1, 0, CAP - 1)
    slot_of = jnp.where(active_flat == 1, jnp.take_along_axis(slot_order, order_index, axis=1), -1)

    def rim_list(row):
        act_row = active[:, row, :]
        rank_row = jnp.cumsum(act_row, axis=1) - 1
        slot_row = slot_of[:, row * RIM:(row + 1) * RIM]
        match = (act_row[:, :, None] == 1) & (rank_row[:, :, None] == jnp.arange(RIM, dtype=jnp.int32)[None, None, :])
        listed = jnp.sum(jnp.where(match, slot_row[:, :, None], 0), axis=1)
        filled = jnp.any(match, axis=1)
        return (jnp.where(filled, listed, CAP).astype(jnp.int32), rank_row, act_row)
    first_list, first_rank, first_act = rim_list(0)
    last_list, last_rank, last_act = rim_list(row_count - 1)
    rim_table = jnp.concatenate([first_list, last_list], axis=1)
    empty_row = jnp.zeros((1, RIM), jnp.int32)
    prev_act = jnp.concatenate([empty_row, last_act[:-1]], axis=0)
    prev_rank = jnp.concatenate([empty_row, last_rank[:-1]], axis=0)
    next_act = jnp.concatenate([first_act[1:], empty_row], axis=0)
    next_rank = jnp.concatenate([first_rank[1:], empty_row], axis=0)
    position = np.arange(row_count * RIM)
    pos_row = position // RIM
    pos_col = position % RIM // 2
    pos_height = position % 2
    columns = []
    for offset in range(27):
        step_row = offset // 9 - 1
        step_col = offset // 3 % 3 - 1
        step_height = offset % 3 - 1
        new_row = pos_row + step_row
        new_col = pos_col + step_col
        new_height = pos_height + step_height
        lateral = (new_col >= 0) & (new_col < 2) & (new_height >= 0) & (new_height < 2)
        in_row = np.clip(new_col, 0, 1) * 2 + np.clip(new_height, 0, 1)
        target = np.clip(new_row, 0, row_count - 1) * RIM + in_row
        local_slot = slot_of[:, target]
        local_ok = jnp.asarray(lateral & (new_row >= 0) & (new_row < row_count)) & (local_slot >= 0)
        prev_ok = jnp.asarray(lateral & (new_row == -1)) & (prev_act[:, in_row] == 1)
        next_ok = jnp.asarray(lateral & (new_row == row_count)) & (next_act[:, in_row] == 1)
        value = jnp.where(local_ok, local_slot, jnp.where(prev_ok, CAP + prev_rank[:, in_row], jnp.where(next_ok, CAP + RIM + next_rank[:, in_row], sentinel)))
        columns.append(value.astype(jnp.int32))
    pos_table = jnp.stack(columns, axis=-1)
    onehot = slot_of[:, :, None] == jnp.arange(CAP, dtype=jnp.int32)[None, None, :]
    table = jnp.sum(jnp.where(onehot[:, :, :, None], pos_table[:, :, None, :], 0), axis=1)
    table = table + jnp.where(jnp.any(onehot, axis=1), 0, sentinel)[:, :, None]
    return (table.reshape(tile_count * CAP, 27).astype(jnp.int32), rim_table)


def draw_nbr_table(key, part):
    return brick_geometry(key)[0]


def draw_rim_slots(key, part):
    return brick_geometry(key)[1]


def block_levels(own_key, extent, cuts, low, high):
    gain = 1.0
    for dim, shards_of in cuts:
        steps = jax.random.uniform(jax.random.fold_in(jax.random.fold_in(own_key, 6), dim), (shards_of,), jnp.float32, low / len(cuts), high / len(cuts))
        gain = gain * jnp.repeat(jnp.exp(steps), extent[dim] // shards_of).reshape((-1,) + (1,) * (len(extent) - 1 - dim))
    return gain


def normal_values(rng, shape, spread, most, shards=(), held_as=jnp.bfloat16):
    level = block_levels(rng, shape, shards, -0.22, 0.18) if shards else 1.0
    values = jax.random.normal(rng, shape, jnp.float32) * spread * level
    return jnp.minimum(jnp.maximum(values, -most), most).astype(held_as)


def setup_inputs(seed: int = 0, part: int = 0) -> dict:
    streams_of = jax.random.split(jax.random.key(seed), 7)
    part_keys = jax.random.split(jax.random.fold_in(streams_of[6], part), 7)
    features = normal_values(part_keys[0], (BRICKS, VOX, C), 1.0, 6.0, ((0, 16),))
    nbr_table = draw_nbr_table(jax.random.fold_in(jax.random.fold_in(streams_of[6], part), 71), part)
    rim_slots = draw_rim_slots(jax.random.fold_in(jax.random.fold_in(streams_of[6], part), 71), part)
    w_first = normal_values(streams_of[3], (KK * C, C), (8 * C) ** -0.5, 0.1875, ((0, 16),))
    w_second = normal_values(streams_of[4], (KK * C, C), (8 * C) ** -0.5, 0.1875, ((0, 16),))
    cotangent = normal_values(part_keys[5], (BRICKS, VOX, C), 0.01, 0.059814453, ((0, 16),))
    return {"features": features, "nbr_table": nbr_table, "rim_slots": rim_slots, "w_first": w_first, "w_second": w_second, "cotangent": cotangent}


def brick_tables(side):
    coords = np.arange(side ** 3)
    first = coords // (side * side)
    second = (coords // side) % side
    third = coords % side
    brick_code = np.zeros((side ** 3, 27), np.int32)
    voxel_code = np.zeros((side ** 3, 27), np.int32)
    for offset in range(27):
        shifts = (offset // 9 - 1, (offset // 3) % 3 - 1, offset % 3 - 1)
        code = np.zeros(side ** 3, np.int32)
        local = np.zeros(side ** 3, np.int32)
        for along, step in zip((first, second, third), shifts):
            moved = along + step
            brick_step = moved // side
            code = code * 3 + brick_step + 1
            local = local * side + moved - brick_step * side
        brick_code[:, offset] = code
        voxel_code[:, offset] = local
    return brick_code, voxel_code


def windows(extended, table, brick_code, voxel_code):
    vox_count = extended.shape[1]
    flat = extended.reshape(-1, extended.shape[2])
    index = table[:, brick_code] * vox_count + jnp.asarray(voxel_code)[None]
    picked = jnp.take(flat, index.reshape(-1).astype(jnp.int32), axis=0)
    return picked.reshape(table.shape[0] * vox_count, -1)


def extend(blocks, rim_slots):
    zero_brick = jnp.zeros((TILES, 1) + blocks.shape[2:], blocks.dtype)
    padded = jnp.concatenate([blocks, zero_brick], axis=1)
    picked = jax.vmap(lambda tile_bricks, chosen: jnp.take(tile_bricks, chosen, axis=0))(padded, rim_slots)
    to_prev = picked[:, :RIM]
    to_next = picked[:, RIM:]
    empty = jnp.zeros((1, RIM) + blocks.shape[2:], blocks.dtype)
    from_prev = jnp.concatenate([empty, to_next[:-1]], axis=0)
    from_next = jnp.concatenate([to_prev[1:], empty], axis=0)
    return jnp.concatenate([blocks, from_prev, from_next, zero_brick], axis=1)


def reference(features, nbr_table, rim_slots, w_first, w_second, cotangent):
    brick_code, voxel_code = brick_tables(BS)
    tile_shape = (TILES, CAP, VOX, C)
    tables = nbr_table.reshape(TILES, CAP, KK)

    def convolve(blocks, weight):
        extended = extend(blocks.reshape(tile_shape), rim_slots)

        def one_tile(pair):
            ext_tile, table = pair
            return jnp.dot(windows(ext_tile, table, brick_code, voxel_code), weight, preferred_element_type=jnp.float32)

        return lax.map(one_tile, (extended, tables))

    first_sum = convolve(features, w_first)
    hidden = jax.nn.silu(first_sum).astype(jnp.bfloat16)
    out_map = convolve(hidden, w_second).astype(jnp.bfloat16).reshape(BRICKS, VOX, C)
    flipped = w_second.reshape(KK, C, C)[::-1].transpose(0, 2, 1).reshape(KK * C, C)
    back = convolve(cotangent, flipped)
    sigmoid_mid = jax.nn.sigmoid(first_sum)
    grad_mid = (back * sigmoid_mid * (1.0 + first_sum * (1.0 - sigmoid_mid))).astype(jnp.bfloat16)
    ext_in = extend(features.reshape(tile_shape), rim_slots)
    ext_mid = extend(hidden.reshape(tile_shape), rim_slots)
    cot_tiles = cotangent.reshape(TILES, CAP * VOX, C)

    def accumulate(carry, items):
        e_in, e_mid, table, cot_rows, mid_rows = items
        left = windows(e_mid, table, brick_code, voxel_code)
        total_second = carry[1] + jnp.dot(left.T, cot_rows, preferred_element_type=jnp.float32)
        right = windows(e_in, table, brick_code, voxel_code)
        total_first = carry[0] + jnp.dot(right.T, mid_rows, preferred_element_type=jnp.float32)
        return (total_first, total_second), None

    start = (jnp.zeros((KK * C, C), jnp.float32), jnp.zeros((KK * C, C), jnp.float32))
    (grad_first, grad_second), _ = lax.scan(accumulate, start, (ext_in, ext_mid, tables, cot_tiles, grad_mid))
    return out_map, grad_first, grad_second
```

```python
import jax
import jax.numpy as jnp
import numpy as np
from jax import lax
from jax.sharding import PartitionSpec as P

BS = 4
SLOTS = 16


def halo_tables(side):
    wide = side + 2
    coords = np.arange(wide**3)
    brick = np.zeros(wide**3, np.int32)
    local = np.zeros(wide**3, np.int32)
    for along in (coords // (wide * wide), coords // wide % wide, coords % wide):
        moved = along - 1
        step = moved // side
        brick = brick * 3 + step + 1
        local = local * side + moved - step * side
    return (brick.astype(np.int32), local.astype(np.int32))


def neighbours(packed, rim_count):
    size = lax.axis_size("tx")
    up = [(i, (i + 1) % size) for i in range(size - 1)]
    down = [(j, i) for i, j in up]
    before = lax.ppermute(packed[:, rim_count:], "tx", up)
    after = lax.ppermute(packed[:, :rim_count], "tx", down)
    return (before, after)


def on_device(features, nbr_table, rim_slots, w_first, w_second, cotangent):
    capacity, vox_count, channels = features.shape
    rim_count = rim_slots.shape[1] // 2
    chosen = rim_slots[0][:, None] == jnp.arange(capacity)[None, :]
    zero_slot = capacity + 2 * rim_count
    width = zero_slot + 4
    brick, local = halo_tables(BS)

    both_w = lax.all_gather(
        jnp.concatenate([w_first, w_second], axis=1), "tx", axis=0, tiled=True
    )

    table = jnp.pad(
        nbr_table, ((0, SLOTS - capacity), (0, 0)), constant_values=zero_slot
    ).T
    index = (jnp.take(table, brick, axis=0) + jnp.asarray(local)[:, None] * width).reshape(-1)

    def halo(blocks):
        live = blocks[:, :capacity]
        packed = jnp.sum(
            jnp.where(chosen[None, :, :, None], live[:, None], 0), axis=2, dtype=jnp.float32
        ).astype(blocks.dtype)
        before, after = neighbours(packed, rim_count)
        extended = jnp.concatenate(
            [
                live,
                before,
                after,
                jnp.zeros((vox_count, width - zero_slot, blocks.shape[2]), blocks.dtype),
            ],
            axis=1,
        )
        picked = jnp.take(
            extended.reshape(-1, blocks.shape[2]), index, axis=0, mode="clip"
        )
        wide = BS + 2
        return picked.reshape(wide, wide, wide, SLOTS, blocks.shape[2])

    def windows(padded):
        parts = []
        for offset in range(27):
            a, b, c = (offset // 9, offset // 3 % 3, offset % 3)
            part = padded[a : a + BS, b : b + BS, c : c + BS]
            parts.append(part.reshape(vox_count * SLOTS, channels))
        return jnp.concatenate(parts, axis=1)

    stacked = jnp.concatenate([features, cotangent], axis=2).transpose(1, 0, 2)
    outer = halo(stacked)
    inputs = windows(outer[..., :channels])
    cots = windows(outer[..., channels:])
    full_first, full_second = (both_w[:, :channels], both_w[:, channels:])
    kernel_count = full_second.shape[0] // channels
    flipped = (
        full_second.reshape(kernel_count, channels, channels)[::-1]
        .transpose(0, 2, 1)
        .reshape(-1, channels)
    )
    first_sum = jnp.dot(inputs, full_first, preferred_element_type=jnp.float32)
    sigmoid_mid = jax.nn.sigmoid(first_sum)
    hidden = (first_sum * sigmoid_mid).astype(jnp.bfloat16)
    back = jnp.dot(cots, flipped, preferred_element_type=jnp.float32)
    grad_mid = (back * sigmoid_mid * (1.0 + first_sum * (1.0 - sigmoid_mid))).astype(jnp.bfloat16)
    contract = (((0,), (0,)), ((), ()))
    term_first = lax.dot_general(inputs, grad_mid, contract, preferred_element_type=jnp.float32)
    grad_first = lax.psum_scatter(term_first, "tx", scatter_dimension=0, tiled=True)

    middle = windows(halo(hidden.reshape(vox_count, SLOTS, channels)))
    out_map = jnp.dot(middle, full_second, preferred_element_type=jnp.float32).astype(jnp.bfloat16)
    out_map = out_map.reshape(vox_count, SLOTS, channels)[:, :capacity].transpose(1, 0, 2)
    cot_rows = jnp.pad(
        stacked[..., channels:], ((0, 0), (0, SLOTS - capacity), (0, 0))
    ).reshape(-1, channels)
    term_second = lax.dot_general(middle, cot_rows, contract, preferred_element_type=jnp.float32)
    grad_second = lax.psum_scatter(term_second, "tx", scatter_dimension=0, tiled=True)
    return (out_map, grad_first, grad_second)


def solution(mesh):
    placed = (
        P(("groups", "tx"), None, None),
        P(("groups", "tx"), None),
        P(("groups", "tx"), None),
        P("tx", None),
        P("tx", None),
        P(("groups", "tx"), None, None),
    )
    return jax.shard_map(
        on_device,
        mesh=mesh,
        in_specs=placed,
        out_specs=(
            P(("groups", "tx"), None, None),
            P(("groups", "tx"), None),
            P(("groups", "tx"), None),
        ),
        check_vma=False,
    )
```

```python
import functools

import jax
import jax.numpy as jnp
import numpy as np
from jax import lax
from jax.experimental import pallas as pl
from jax.experimental.pallas import tpu as pltpu
from jax.sharding import PartitionSpec as P

BS = 4
SLOTS = 16


def halo_tables(side):
    wide = side + 2
    coords = np.arange(wide**3)
    brick = np.zeros(wide**3, np.int32)
    local = np.zeros(wide**3, np.int32)
    for along in (coords // (wide * wide), coords // wide % wide, coords % wide):
        moved = along - 1
        step = moved // side
        brick = brick * 3 + step + 1
        local = local * side + moved - step * side
    return (brick.astype(np.int32), local.astype(np.int32))


def neighbours(packed, rim_count):
    size = lax.axis_size("tx")
    up = [(i, (i + 1) % size) for i in range(size - 1)]
    down = [(j, i) for i, j in up]
    before = lax.ppermute(packed[:, rim_count:], "tx", up)
    after = lax.ppermute(packed[:, :rim_count], "tx", down)
    return (before, after)


def bit_orders(size):
    count = size.bit_length() - 1
    middle = 1 + (count - 1) // 2
    rest = list(range(middle, count)) + list(range(1, middle))
    return (list(range(count)), [0] + rest)


def halving_kernel(size, orders, first, second, out_first, out_second, *scratch):
    steps = size.bit_length() - 1
    sends, recvs, sums = (scratch[: 2 * steps], scratch[2 * steps : 4 * steps], scratch[4 * steps : -2])
    send_sem, recv_sem = scratch[-2:]
    me = lax.axis_index("tx")
    barrier = pltpu.get_barrier_semaphore()

    def bit_of(bit):
        return me // (1 << bit) % 2

    def partner(bit):
        return me + (1 - 2 * bit_of(bit)) * (1 << bit)

    for bit in range(steps):
        pl.semaphore_signal(
            barrier, inc=1, device_id={"tx": partner(bit)}, device_id_type=pl.DeviceIdType.MESH
        )
    pl.semaphore_wait(barrier, steps)

    held = [lambda i: first[i], lambda i: second[i]]
    left = [list(range(steps)), list(range(steps))]
    copies = [[], []]
    outs = (out_first, out_second)
    for step in range(steps + 1):
        for stream in range(2):
            if step:
                arrived = recvs[stream * steps + step - 1]
                copies[stream][-1].wait_recv()
                kept = keep[stream]

                def read(i, kept=kept, arrived=arrived):
                    return kept(i) + arrived[i].astype(jnp.float32)

            else:
                read = held[stream]
                if stream == 0:
                    keep = [None, None]
            if step == steps:
                outs[stream][...] = read(0)
                continue
            bit = orders[stream][step]
            low = 1 << left[stream].index(bit)
            left[stream].remove(bit)
            half = size >> (step + 1)
            mine = bit_of(bit)

            def entry(j, side, low=low):
                return j // low * (2 * low) + side * low + j % low

            out = sends[stream * steps + step]

            def pack(j, carry, out=out, read=read, entry=entry, mine=mine):
                out[j] = read(entry(j, 1 - mine)).astype(out.dtype)
                return carry

            lax.fori_loop(0, half, pack, 0)
            copy = pltpu.make_async_remote_copy(
                src_ref=out,
                dst_ref=recvs[stream * steps + step],
                send_sem=send_sem.at[stream, step],
                recv_sem=recv_sem.at[stream, step],
                device_id={"tx": partner(bit)},
                device_id_type=pl.DeviceIdType.MESH,
            )
            copy.start()
            copies[stream].append(copy)
            total = sums[stream * steps + step]

            def fold(j, carry, total=total, read=read, entry=entry, mine=mine):
                total[j] = read(entry(j, mine))
                return carry

            lax.fori_loop(0, half, fold, 0)
            keep[stream] = lambda i, total=total: total[i]
    for stream in range(2):
        for copy in copies[stream]:
            copy.wait_send()


def reduce_both(first, second):
    size = lax.axis_size("tx")
    steps = size.bit_length() - 1
    rows = first.shape[0] // size
    tall = -(-rows // 16) * 16
    lanes = first.shape[1]
    first, second = (
        jnp.pad(x.reshape(size, rows, lanes), ((0, 0), (0, tall - rows), (0, 0)))
        for x in (first, second)
    )
    halves = [(size >> (step + 1), tall, lanes) for step in range(steps)] * 2
    whole = pl.BlockSpec(memory_space=pltpu.VMEM)
    outs = pl.pallas_call(
        functools.partial(halving_kernel, size, bit_orders(size)),
        out_shape=[jax.ShapeDtypeStruct((tall, lanes), jnp.float32)] * 2,
        in_specs=[whole] * 2,
        out_specs=[whole] * 2,
        scratch_shapes=[pltpu.VMEM(shape, jnp.bfloat16) for shape in halves * 2]
        + [pltpu.VMEM(shape, jnp.float32) for shape in halves]
        + [pltpu.SemaphoreType.DMA((2, steps)), pltpu.SemaphoreType.DMA((2, steps))],
        compiler_params=pltpu.CompilerParams(
            collective_id=0, has_side_effects=True, vmem_limit_bytes=32 * 1024 * 1024
        ),
    )(first, second)
    return [x[:rows] for x in outs]


def on_device(features, nbr_table, rim_slots, w_first, w_second, cotangent):
    capacity, vox_count, channels = features.shape
    rim_count = rim_slots.shape[1] // 2
    chosen = rim_slots[0][:, None] == jnp.arange(capacity)[None, :]
    zero_slot = capacity + 2 * rim_count
    width = zero_slot + 4
    brick, local = halo_tables(BS)

    both_w = lax.all_gather(
        jnp.concatenate([w_first, w_second], axis=1), "tx", axis=0, tiled=True
    )

    table = jnp.pad(
        nbr_table, ((0, SLOTS - capacity), (0, 0)), constant_values=zero_slot
    ).T
    index = (jnp.take(table, brick, axis=0) + jnp.asarray(local)[:, None] * width).reshape(-1)

    def halo(blocks):
        live = blocks[:, :capacity]
        packed = jnp.sum(
            jnp.where(chosen[None, :, :, None], live[:, None], 0), axis=2, dtype=jnp.float32
        ).astype(blocks.dtype)
        before, after = neighbours(packed, rim_count)
        extended = jnp.concatenate(
            [
                live,
                before,
                after,
                jnp.zeros((vox_count, width - zero_slot, blocks.shape[2]), blocks.dtype),
            ],
            axis=1,
        )
        picked = jnp.take(
            extended.reshape(-1, blocks.shape[2]), index, axis=0, mode="clip"
        )
        wide = BS + 2
        return picked.reshape(wide, wide, wide, SLOTS, blocks.shape[2])

    def windows(padded):
        parts = []
        for offset in range(27):
            a, b, c = (offset // 9, offset // 3 % 3, offset % 3)
            part = padded[a : a + BS, b : b + BS, c : c + BS]
            parts.append(part.reshape(vox_count * SLOTS, channels))
        return jnp.concatenate(parts, axis=1)

    stacked = jnp.concatenate([features, cotangent], axis=2).transpose(1, 0, 2)
    outer = halo(stacked)
    inputs = windows(outer[..., :channels])
    cots = windows(outer[..., channels:])
    full_first, full_second = (both_w[:, :channels], both_w[:, channels:])
    kernel_count = full_second.shape[0] // channels
    flipped = (
        full_second.reshape(kernel_count, channels, channels)[::-1]
        .transpose(0, 2, 1)
        .reshape(-1, channels)
    )
    first_sum = jnp.dot(inputs, full_first, preferred_element_type=jnp.float32)
    sigmoid_mid = jax.nn.sigmoid(first_sum)
    hidden = (first_sum * sigmoid_mid).astype(jnp.bfloat16)
    back = jnp.dot(cots, flipped, preferred_element_type=jnp.float32)
    grad_mid = (back * sigmoid_mid * (1.0 + first_sum * (1.0 - sigmoid_mid))).astype(jnp.bfloat16)
    contract = (((0,), (0,)), ((), ()))
    term_first = lax.dot_general(inputs, grad_mid, contract, preferred_element_type=jnp.float32)

    middle = windows(halo(hidden.reshape(vox_count, SLOTS, channels)))
    out_map = jnp.dot(middle, full_second, preferred_element_type=jnp.float32).astype(jnp.bfloat16)
    out_map = out_map.reshape(vox_count, SLOTS, channels)[:, :capacity].transpose(1, 0, 2)
    cot_rows = jnp.pad(
        stacked[..., channels:], ((0, 0), (0, SLOTS - capacity), (0, 0))
    ).reshape(-1, channels)
    term_second = lax.dot_general(middle, cot_rows, contract, preferred_element_type=jnp.float32)
    grad_first, grad_second = reduce_both(term_first, term_second)
    return (out_map, grad_first, grad_second)


def solution(mesh):
    placed = (
        P(("groups", "tx"), None, None),
        P(("groups", "tx"), None),
        P(("groups", "tx"), None),
        P("tx", None),
        P("tx", None),
        P(("groups", "tx"), None, None),
    )
    return jax.shard_map(
        on_device,
        mesh=mesh,
        in_specs=placed,
        out_specs=(
            P(("groups", "tx"), None, None),
            P(("groups", "tx"), None),
            P(("groups", "tx"), None),
        ),
        check_vma=False,
    )
```

```python
import functools

import jax
import jax.numpy as jnp
import numpy as np
from jax import lax
from jax.experimental import pallas as pl
from jax.experimental.pallas import tpu as pltpu
from jax.sharding import PartitionSpec as P

BS = 4
SLOTS = 16


def halo_tables(side):
    wide = side + 2
    coords = np.arange(wide**3)
    brick = np.zeros(wide**3, np.int32)
    local = np.zeros(wide**3, np.int32)
    for along in (coords // (wide * wide), coords // wide % wide, coords % wide):
        moved = along - 1
        step = moved // side
        brick = brick * 3 + step + 1
        local = local * side + moved - step * side
    return (brick.astype(np.int32), local.astype(np.int32))


def neighbours(packed, rim_count):
    size = lax.axis_size("tx")
    up = [(i, (i + 1) % size) for i in range(size - 1)]
    down = [(j, i) for i, j in up]
    before = lax.ppermute(packed[:, rim_count:], "tx", up)
    after = lax.ppermute(packed[:, :rim_count], "tx", down)
    return (before, after)


def bit_orders(size):
    count = size.bit_length() - 1
    middle = 1 + (count - 1) // 2
    rest = list(range(middle, count)) + list(range(1, middle))
    return (list(range(count)), [0] + rest)


def halving_kernel(size, orders, first, second, out_first, out_second, *scratch):
    steps = size.bit_length() - 1
    sends, recvs, sums = (scratch[: 2 * steps], scratch[2 * steps : 4 * steps], scratch[4 * steps : -2])
    send_sem, recv_sem = scratch[-2:]
    me = lax.axis_index("tx")
    barrier = pltpu.get_barrier_semaphore()

    def bit_of(bit):
        return me // (1 << bit) % 2

    def partner(bit):
        return me + (1 - 2 * bit_of(bit)) * (1 << bit)

    for bit in range(steps):
        pl.semaphore_signal(
            barrier, inc=1, device_id={"tx": partner(bit)}, device_id_type=pl.DeviceIdType.MESH
        )
    pl.semaphore_wait(barrier, steps)

    held = [lambda i: first[i], lambda i: second[i]]
    left = [list(range(steps)), list(range(steps))]
    copies = [[], []]
    outs = (out_first, out_second)
    for step in range(steps + 1):
        for stream in range(2):
            if step:
                arrived = recvs[stream * steps + step - 1]
                copies[stream][-1].wait_recv()
                kept = keep[stream]

                def read(i, kept=kept, arrived=arrived):
                    return kept(i) + arrived[i].astype(jnp.float32)

            else:
                read = held[stream]
                if stream == 0:
                    keep = [None, None]
            if step == steps:
                outs[stream][...] = read(0)
                continue
            bit = orders[stream][step]
            low = 1 << left[stream].index(bit)
            left[stream].remove(bit)
            half = size >> (step + 1)
            mine = bit_of(bit)

            def entry(j, side, low=low):
                return j // low * (2 * low) + side * low + j % low

            out = sends[stream * steps + step]

            def pack(j, carry, out=out, read=read, entry=entry, mine=mine):
                out[j] = read(entry(j, 1 - mine)).astype(out.dtype)
                return carry

            lax.fori_loop(0, half, pack, 0)
            copy = pltpu.make_async_remote_copy(
                src_ref=out,
                dst_ref=recvs[stream * steps + step],
                send_sem=send_sem.at[stream, step],
                recv_sem=recv_sem.at[stream, step],
                device_id={"tx": partner(bit)},
                device_id_type=pl.DeviceIdType.MESH,
            )
            copy.start()
            copies[stream].append(copy)
            total = sums[stream * steps + step]

            def fold(j, carry, total=total, read=read, entry=entry, mine=mine):
                total[j] = read(entry(j, mine))
                return carry

            lax.fori_loop(0, half, fold, 0)
            keep[stream] = lambda i, total=total: total[i]
    for stream in range(2):
        for copy in copies[stream]:
            copy.wait_send()


def reduce_both(first, second):
    size = lax.axis_size("tx")
    steps = size.bit_length() - 1
    rows = first.shape[0] // size
    tall = -(-rows // 16) * 16
    lanes = first.shape[1]
    first, second = (
        jnp.pad(x.reshape(size, rows, lanes), ((0, 0), (0, tall - rows), (0, 0)))
        for x in (first, second)
    )
    halves = [(size >> (step + 1), tall, lanes) for step in range(steps)] * 2
    whole = pl.BlockSpec(memory_space=pltpu.VMEM)
    outs = pl.pallas_call(
        functools.partial(halving_kernel, size, bit_orders(size)),
        out_shape=[jax.ShapeDtypeStruct((tall, lanes), jnp.float32)] * 2,
        in_specs=[whole] * 2,
        out_specs=[whole] * 2,
        scratch_shapes=[pltpu.VMEM(shape, jnp.bfloat16) for shape in halves * 2]
        + [pltpu.VMEM(shape, jnp.float32) for shape in halves]
        + [pltpu.SemaphoreType.DMA((2, steps)), pltpu.SemaphoreType.DMA((2, steps))],
        compiler_params=pltpu.CompilerParams(
            collective_id=0, has_side_effects=True, vmem_limit_bytes=32 * 1024 * 1024
        ),
    )(first, second)
    return [x[:rows] for x in outs]


CONTRACT = (((0,), (0,)), ((), ()))


def fill_windows(win, padded):
    channels = padded.shape[-1]
    for offset in range(27):
        a, b, c = (offset // 9, offset // 3 % 3, offset % 3)
        for i in range(BS):
            part = padded[a + i, b : b + BS, c : c + BS]
            rows = BS * BS * SLOTS
            win[i * rows : (i + 1) * rows, offset * channels : (offset + 1) * channels] = (
                part.reshape(rows, channels)
            )


def row_tiles(win, body):
    rows = BS * BS * SLOTS

    def step(i, carry):
        body(pl.ds(pl.multiple_of(i * rows, rows), rows))
        return carry

    lax.fori_loop(0, win.shape[0] // rows, step, 0)


def kernel_gradient(win, cots, term):
    channels = term.shape[1]
    wide = 3 * channels

    def step(i, carry):
        columns = pl.ds(pl.multiple_of(i * wide, wide), wide)
        term[columns, :] = lax.dot_general(
            win[:, columns], cots[...], CONTRACT, preferred_element_type=jnp.float32
        )
        return carry

    lax.fori_loop(0, win.shape[1] // wide, step, 0)


def first_kernel(feats, cots, w_first, flipped, hidden, term, win, back, grad_mid):
    fill_windows(win, cots)

    def backward(rows):
        back[rows, :] = jnp.dot(win[rows, :], flipped[...], preferred_element_type=jnp.float32)

    row_tiles(win, backward)
    fill_windows(win, feats)

    def forward(rows):
        first_sum = jnp.dot(win[rows, :], w_first[...], preferred_element_type=jnp.float32)
        gate = jax.nn.sigmoid(first_sum)
        hidden[rows, :] = (first_sum * gate).astype(hidden.dtype)
        grad_mid[rows, :] = (
            back[rows, :] * gate * (1.0 + first_sum * (1.0 - gate))
        ).astype(grad_mid.dtype)

    row_tiles(win, forward)
    kernel_gradient(win, grad_mid, term)


def second_kernel(mids, cots, w_second, out_map, term, win):
    fill_windows(win, mids)

    def forward(rows):
        out_map[rows, :] = jnp.dot(
            win[rows, :], w_second[...], preferred_element_type=jnp.float32
        ).astype(out_map.dtype)

    row_tiles(win, forward)
    kernel_gradient(win, cots, term)


def local_call(body, operands, extra):
    depth, channels = operands[2].shape
    rows = BS**3 * SLOTS
    whole = pl.BlockSpec(memory_space=pltpu.VMEM)
    return pl.pallas_call(
        body,
        out_shape=[
            jax.ShapeDtypeStruct((rows, channels), jnp.bfloat16),
            jax.ShapeDtypeStruct((depth, channels), jnp.float32),
        ],
        in_specs=[whole] * len(operands),
        out_specs=[whole] * 2,
        scratch_shapes=[pltpu.VMEM((rows, depth), jnp.bfloat16)]
        + [pltpu.VMEM((rows, channels), kind) for kind in extra],
        compiler_params=pltpu.CompilerParams(vmem_limit_bytes=40 * 1024 * 1024),
    )(*operands)


def on_device(features, nbr_table, rim_slots, w_first, w_second, cotangent):
    capacity, vox_count, channels = features.shape
    rim_count = rim_slots.shape[1] // 2
    chosen = rim_slots[0][:, None] == jnp.arange(capacity)[None, :]
    zero_slot = capacity + 2 * rim_count
    width = zero_slot + 4
    brick, local = halo_tables(BS)

    own_w, features, cotangent = lax.optimization_barrier(
        (jnp.concatenate([w_first, w_second], axis=1), features, cotangent)
    )
    both_w = lax.all_gather(own_w, "tx", axis=0, tiled=True)

    table = jnp.pad(
        nbr_table, ((0, SLOTS - capacity), (0, 0)), constant_values=zero_slot
    ).T
    index = (jnp.take(table, brick, axis=0) + jnp.asarray(local)[:, None] * width).reshape(-1)

    def halo(blocks):
        live = blocks[:, :capacity]
        packed = jnp.sum(
            jnp.where(chosen[None, :, :, None], live[:, None], 0), axis=2, dtype=jnp.float32
        ).astype(blocks.dtype)
        before, after = neighbours(packed, rim_count)
        extended = jnp.concatenate(
            [
                live,
                before,
                after,
                jnp.zeros((vox_count, width - zero_slot, blocks.shape[2]), blocks.dtype),
            ],
            axis=1,
        )
        picked = jnp.take(
            extended.reshape(-1, blocks.shape[2]), index, axis=0, mode="clip"
        )
        wide = BS + 2
        return picked.reshape(wide, wide, wide, SLOTS, blocks.shape[2])

    stacked = jnp.concatenate([features, cotangent], axis=2).transpose(1, 0, 2)
    outer = halo(stacked)
    full_first, full_second = (both_w[:, :channels], both_w[:, channels:])
    kernel_count = full_second.shape[0] // channels
    flipped = (
        full_second.reshape(kernel_count, channels, channels)[::-1]
        .transpose(0, 2, 1)
        .reshape(-1, channels)
    )
    hidden, term_first = local_call(
        first_kernel,
        (outer[..., :channels], outer[..., channels:], full_first, flipped),
        (jnp.float32, jnp.bfloat16),
    )
    cot_rows = jnp.pad(
        stacked[..., channels:], ((0, 0), (0, SLOTS - capacity), (0, 0))
    ).reshape(-1, channels)
    middle = halo(hidden.reshape(vox_count, SLOTS, channels))
    out_map, term_second = local_call(second_kernel, (middle, cot_rows, full_second), ())
    out_map = out_map.reshape(vox_count, SLOTS, channels)[:, :capacity].transpose(1, 0, 2)
    grad_first, grad_second = reduce_both(term_first, term_second)
    return (out_map, grad_first, grad_second)


def solution(mesh):
    placed = (
        P(("groups", "tx"), None, None),
        P(("groups", "tx"), None),
        P(("groups", "tx"), None),
        P("tx", None),
        P("tx", None),
        P(("groups", "tx"), None, None),
    )
    return jax.shard_map(
        on_device,
        mesh=mesh,
        in_specs=placed,
        out_specs=(
            P(("groups", "tx"), None, None),
            P(("groups", "tx"), None),
            P(("groups", "tx"), None),
        ),
        check_vma=False,
    )
```

```python
import functools

import jax
import jax.numpy as jnp
import numpy as np
from jax import lax
from jax.experimental import pallas as pl
from jax.experimental.pallas import tpu as pltpu
from jax.sharding import PartitionSpec as P

BS = 4
SLOTS = 16


def halo_tables(side):
    wide = side + 2
    coords = np.arange(wide**3)
    brick = np.zeros(wide**3, np.int32)
    local = np.zeros(wide**3, np.int32)
    for along in (coords // (wide * wide), coords // wide % wide, coords % wide):
        moved = along - 1
        step = moved // side
        brick = brick * 3 + step + 1
        local = local * side + moved - step * side
    return (brick.astype(np.int32), local.astype(np.int32))


def neighbours(packed, rim_count):
    size = lax.axis_size("tx")
    up = [(i, (i + 1) % size) for i in range(size - 1)]
    down = [(j, i) for i, j in up]
    before = lax.ppermute(packed[:, rim_count:], "tx", up)
    after = lax.ppermute(packed[:, :rim_count], "tx", down)
    return (before, after)


def bit_orders(size):
    count = size.bit_length() - 1
    middle = 1 + (count - 1) // 2
    rest = list(range(middle, count)) + list(range(1, middle))
    return (list(range(count)), [0] + rest)


def halving_kernel(size, orders, first, second, out_first, out_second, *scratch):
    steps = size.bit_length() - 1
    sends, recvs, sums = (scratch[: 2 * steps], scratch[2 * steps : 4 * steps], scratch[4 * steps : -2])
    send_sem, recv_sem = scratch[-2:]
    me = lax.axis_index("tx")
    barrier = pltpu.get_barrier_semaphore()

    def bit_of(bit):
        return me // (1 << bit) % 2

    def partner(bit):
        return me + (1 - 2 * bit_of(bit)) * (1 << bit)

    for bit in range(steps):
        pl.semaphore_signal(
            barrier, inc=1, device_id={"tx": partner(bit)}, device_id_type=pl.DeviceIdType.MESH
        )
    pl.semaphore_wait(barrier, steps)

    held = [lambda i: first[i], lambda i: second[i]]
    left = [list(range(steps)), list(range(steps))]
    copies = [[], []]
    outs = (out_first, out_second)
    for step in range(steps + 1):
        for stream in range(2):
            if step:
                arrived = recvs[stream * steps + step - 1]
                copies[stream][-1].wait_recv()
                kept = keep[stream]

                def read(i, kept=kept, arrived=arrived):
                    return kept(i) + arrived[i].astype(jnp.float32)

            else:
                read = held[stream]
                if stream == 0:
                    keep = [None, None]
            if step == steps:
                outs[stream][...] = read(0)
                continue
            bit = orders[stream][step]
            low = 1 << left[stream].index(bit)
            left[stream].remove(bit)
            half = size >> (step + 1)
            mine = bit_of(bit)

            def entry(j, side, low=low):
                return j // low * (2 * low) + side * low + j % low

            out = sends[stream * steps + step]

            def pack(j, carry, out=out, read=read, entry=entry, mine=mine):
                out[j] = read(entry(j, 1 - mine)).astype(out.dtype)
                return carry

            lax.fori_loop(0, half, pack, 0)
            copy = pltpu.make_async_remote_copy(
                src_ref=out,
                dst_ref=recvs[stream * steps + step],
                send_sem=send_sem.at[stream, step],
                recv_sem=recv_sem.at[stream, step],
                device_id={"tx": partner(bit)},
                device_id_type=pl.DeviceIdType.MESH,
            )
            copy.start()
            copies[stream].append(copy)
            total = sums[stream * steps + step]

            def fold(j, carry, total=total, read=read, entry=entry, mine=mine):
                total[j] = read(entry(j, mine))
                return carry

            lax.fori_loop(0, half, fold, 0)
            keep[stream] = lambda i, total=total: total[i]
    for stream in range(2):
        for copy in copies[stream]:
            copy.wait_send()


def reduce_both(first, second):
    size = lax.axis_size("tx")
    steps = size.bit_length() - 1
    rows = first.shape[0] // size
    tall = -(-rows // 16) * 16
    lanes = first.shape[1]
    first, second = (
        jnp.pad(x.reshape(size, rows, lanes), ((0, 0), (0, tall - rows), (0, 0)))
        for x in (first, second)
    )
    halves = [(size >> (step + 1), tall, lanes) for step in range(steps)] * 2
    whole = pl.BlockSpec(memory_space=pltpu.VMEM)
    outs = pl.pallas_call(
        functools.partial(halving_kernel, size, bit_orders(size)),
        out_shape=[jax.ShapeDtypeStruct((tall, lanes), jnp.float32)] * 2,
        in_specs=[whole] * 2,
        out_specs=[whole] * 2,
        scratch_shapes=[pltpu.VMEM(shape, jnp.bfloat16) for shape in halves * 2]
        + [pltpu.VMEM(shape, jnp.float32) for shape in halves]
        + [pltpu.SemaphoreType.DMA((2, steps)), pltpu.SemaphoreType.DMA((2, steps))],
        compiler_params=pltpu.CompilerParams(
            collective_id=0, has_side_effects=True, vmem_limit_bytes=32 * 1024 * 1024
        ),
    )(first, second)
    return [x[:rows] for x in outs]


CONTRACT = (((0,), (0,)), ((), ()))


def fill_windows(win, padded):
    channels = padded.shape[-1]
    for offset in range(27):
        a, b, c = (offset // 9, offset // 3 % 3, offset % 3)
        for i in range(BS):
            part = padded[a + i, b : b + BS, c : c + BS]
            rows = BS * BS * SLOTS
            win[i * rows : (i + 1) * rows, offset * channels : (offset + 1) * channels] = (
                part.reshape(rows, channels)
            )


def row_tiles(win, body):
    rows = BS * BS * SLOTS

    def step(i, carry):
        body(pl.ds(pl.multiple_of(i * rows, rows), rows))
        return carry

    lax.fori_loop(0, win.shape[0] // rows, step, 0)


def kernel_gradient(win, cots, term):
    channels = term.shape[1]
    wide = 3 * channels

    def step(i, carry):
        columns = pl.ds(pl.multiple_of(i * wide, wide), wide)
        term[columns, :] = lax.dot_general(
            win[:, columns], cots[...], CONTRACT, preferred_element_type=jnp.float32
        )
        return carry

    lax.fori_loop(0, win.shape[1] // wide, step, 0)


def first_kernel(feats, cots, both_w, hidden, term, win, back, grad_mid, flipped):
    channels = term.shape[1]
    for offset in range(27):
        flipped[offset * channels : (offset + 1) * channels, :] = both_w[
            (26 - offset) * channels : (27 - offset) * channels, channels:
        ].T
    fill_windows(win, cots)

    def backward(rows):
        back[rows, :] = jnp.dot(win[rows, :], flipped[...], preferred_element_type=jnp.float32)

    row_tiles(win, backward)
    fill_windows(win, feats)

    def forward(rows):
        first_sum = jnp.dot(win[rows, :], both_w[:, :channels], preferred_element_type=jnp.float32)
        gate = jax.nn.sigmoid(first_sum)
        hidden[rows, :] = (first_sum * gate).astype(hidden.dtype)
        grad_mid[rows, :] = (
            back[rows, :] * gate * (1.0 + first_sum * (1.0 - gate))
        ).astype(grad_mid.dtype)

    row_tiles(win, forward)
    kernel_gradient(win, grad_mid, term)


def fill_halo(padded, extended, choose):
    wide = BS + 2
    brick, local = halo_tables(BS)
    for voxel in range(BS**3):
        places = [p for p in range(wide**3) if local[p] == voxel]
        rows = jnp.concatenate([choose[int(brick[p])] for p in places], axis=0)
        got = jnp.dot(rows, extended[voxel], preferred_element_type=jnp.float32)
        for k, p in enumerate(places):
            padded[p // (wide * wide), p // wide % wide, p % wide] = got[
                k * SLOTS : (k + 1) * SLOTS
            ].astype(padded.dtype)


def second_kernel(extended, cots, both_w, choose, out_map, term, win, padded):
    channels = term.shape[1]
    fill_halo(padded, extended, choose)
    fill_windows(win, padded)

    def forward(rows):
        out_map[rows, :] = jnp.dot(
            win[rows, :], both_w[:, channels:], preferred_element_type=jnp.float32
        ).astype(out_map.dtype)

    row_tiles(win, forward)
    kernel_gradient(win, cots, term)


def local_call(body, operands, extra):
    depth = operands[2].shape[0]
    channels = operands[2].shape[1] // 2
    rows = BS**3 * SLOTS
    whole = pl.BlockSpec(memory_space=pltpu.VMEM)
    return pl.pallas_call(
        body,
        out_shape=[
            jax.ShapeDtypeStruct((rows, channels), jnp.bfloat16),
            jax.ShapeDtypeStruct((depth, channels), jnp.float32),
        ],
        in_specs=[whole] * len(operands),
        out_specs=[whole] * 2,
        scratch_shapes=[pltpu.VMEM((rows, depth), jnp.bfloat16)]
        + [pltpu.VMEM(shape, kind) for shape, kind in extra],
        compiler_params=pltpu.CompilerParams(vmem_limit_bytes=40 * 1024 * 1024),
    )(*operands)


def on_device(features, nbr_table, rim_slots, w_first, w_second, cotangent):
    capacity, vox_count, channels = features.shape
    rim_count = rim_slots.shape[1] // 2
    chosen = rim_slots[0][:, None] == jnp.arange(capacity)[None, :]
    zero_slot = capacity + 2 * rim_count
    width = -(-(zero_slot + 1) // 16) * 16
    brick, local = halo_tables(BS)

    own_w, features, cotangent = lax.optimization_barrier(
        (jnp.concatenate([w_first, w_second], axis=1), features, cotangent)
    )
    both_w = lax.all_gather(own_w, "tx", axis=0, tiled=True)

    table = jnp.pad(
        nbr_table, ((0, SLOTS - capacity), (0, 0)), constant_values=zero_slot
    ).T
    index = (jnp.take(table, brick, axis=0) + jnp.asarray(local)[:, None] * width).reshape(-1)

    def extend(blocks):
        live = blocks[:, :capacity]
        packed = jnp.sum(
            jnp.where(chosen[None, :, :, None], live[:, None], 0), axis=2, dtype=jnp.float32
        ).astype(blocks.dtype)
        before, after = neighbours(packed, rim_count)
        extended = jnp.concatenate(
            [
                live,
                before,
                after,
                jnp.zeros((vox_count, width - zero_slot, blocks.shape[2]), blocks.dtype),
            ],
            axis=1,
        )
        return extended

    stacked = jnp.concatenate([features, cotangent], axis=2).transpose(1, 0, 2)
    wide = BS + 2
    outer = jnp.take(
        extend(stacked).reshape(-1, 2 * channels), index, axis=0, mode="clip"
    ).reshape(wide, wide, wide, SLOTS, 2 * channels)
    rows = vox_count * SLOTS
    hidden, term_first = local_call(
        first_kernel,
        (outer[..., :channels], outer[..., channels:], both_w),
        (
            ((rows, channels), jnp.float32),
            ((rows, channels), jnp.bfloat16),
            ((both_w.shape[0], channels), jnp.bfloat16),
        ),
    )
    cot_rows = jnp.pad(
        stacked[..., channels:], ((0, 0), (0, SLOTS - capacity), (0, 0))
    ).reshape(-1, channels)
    choose = (table[:, :, None] == jnp.arange(width)).astype(jnp.bfloat16)
    out_map, term_second = local_call(
        second_kernel,
        (extend(hidden.reshape(vox_count, SLOTS, channels)), cot_rows, both_w, choose),
        (((wide, wide, wide, SLOTS, channels), jnp.bfloat16),),
    )
    out_map = out_map.reshape(vox_count, SLOTS, channels)[:, :capacity].transpose(1, 0, 2)
    grad_first, grad_second = reduce_both(term_first, term_second)
    return (out_map, grad_first, grad_second)


def solution(mesh):
    placed = (
        P(("groups", "tx"), None, None),
        P(("groups", "tx"), None),
        P(("groups", "tx"), None),
        P("tx", None),
        P("tx", None),
        P(("groups", "tx"), None, None),
    )
    return jax.shard_map(
        on_device,
        mesh=mesh,
        in_specs=placed,
        out_specs=(
            P(("groups", "tx"), None, None),
            P(("groups", "tx"), None),
            P(("groups", "tx"), None),
        ),
        check_vma=False,
    )
```

```python
import functools

import jax
import jax.numpy as jnp
import numpy as np
from jax import lax
from jax.experimental import pallas as pl
from jax.experimental.pallas import tpu as pltpu
from jax.sharding import PartitionSpec as P

BS = 4
SLOTS = 16


def halo_tables(side):
    wide = side + 2
    coords = np.arange(wide**3)
    brick = np.zeros(wide**3, np.int32)
    local = np.zeros(wide**3, np.int32)
    for along in (coords // (wide * wide), coords // wide % wide, coords % wide):
        moved = along - 1
        step = moved // side
        brick = brick * 3 + step + 1
        local = local * side + moved - step * side
    return (brick.astype(np.int32), local.astype(np.int32))


def neighbours(packed, rim_count):
    size = lax.axis_size("tx")
    up = [(i, (i + 1) % size) for i in range(size - 1)]
    down = [(j, i) for i, j in up]
    before = lax.ppermute(packed[:, rim_count:], "tx", up)
    after = lax.ppermute(packed[:, :rim_count], "tx", down)
    return (before, after)


def bit_orders(size):
    count = size.bit_length() - 1
    middle = 1 + (count - 1) // 2
    rest = list(range(middle, count)) + list(range(1, middle))
    return (list(range(count)), [0] + rest)


def halving_kernel(size, orders, first, second, out_first, out_second, *scratch):
    steps = size.bit_length() - 1
    sends, recvs, sums = (scratch[: 2 * steps], scratch[2 * steps : 4 * steps], scratch[4 * steps : -2])
    send_sem, recv_sem = scratch[-2:]
    me = lax.axis_index("tx")
    barrier = pltpu.get_barrier_semaphore()

    def bit_of(bit):
        return me // (1 << bit) % 2

    def partner(bit):
        return me + (1 - 2 * bit_of(bit)) * (1 << bit)

    for bit in range(steps):
        pl.semaphore_signal(
            barrier, inc=1, device_id={"tx": partner(bit)}, device_id_type=pl.DeviceIdType.MESH
        )
    pl.semaphore_wait(barrier, steps)

    held = [lambda i: first[i], lambda i: second[i]]
    left = [list(range(steps)), list(range(steps))]
    copies = [[], []]
    outs = (out_first, out_second)
    for step in range(steps + 1):
        for stream in range(2):
            if step:
                arrived = recvs[stream * steps + step - 1]
                copies[stream][-1].wait_recv()
                kept = keep[stream]

                def read(i, kept=kept, arrived=arrived):
                    return kept(i) + arrived[i].astype(jnp.float32)

            else:
                read = held[stream]
                if stream == 0:
                    keep = [None, None]
            if step == steps:
                outs[stream][...] = read(0)
                continue
            bit = orders[stream][step]
            low = 1 << left[stream].index(bit)
            left[stream].remove(bit)
            half = size >> (step + 1)
            mine = bit_of(bit)

            def entry(j, side, low=low):
                return j // low * (2 * low) + side * low + j % low

            out = sends[stream * steps + step]

            def pack(j, carry, out=out, read=read, entry=entry, mine=mine):
                out[j] = read(entry(j, 1 - mine)).astype(out.dtype)
                return carry

            lax.fori_loop(0, half, pack, 0)
            copy = pltpu.make_async_remote_copy(
                src_ref=out,
                dst_ref=recvs[stream * steps + step],
                send_sem=send_sem.at[stream, step],
                recv_sem=recv_sem.at[stream, step],
                device_id={"tx": partner(bit)},
                device_id_type=pl.DeviceIdType.MESH,
            )
            copy.start()
            copies[stream].append(copy)
            total = sums[stream * steps + step]

            def fold(j, carry, total=total, read=read, entry=entry, mine=mine):
                total[j] = read(entry(j, mine))
                return carry

            lax.fori_loop(0, half, fold, 0)
            keep[stream] = lambda i, total=total: total[i]
    for stream in range(2):
        for copy in copies[stream]:
            copy.wait_send()


def doubling_kernel(size, orders, first, second, out_first, out_second, send_sem, recv_sem):
    steps = size.bit_length() - 1
    me = lax.axis_index("tx")
    barrier = pltpu.get_barrier_semaphore()

    def moved(mask):
        place = me
        for bit in range(steps):
            if mask >> bit & 1:
                place = place + (1 - 2 * (me // (1 << bit) % 2)) * (1 << bit)
        return place

    out_first[me] = first[...]
    out_second[me] = second[...]
    for bit in range(steps):
        pl.semaphore_signal(
            barrier, inc=1, device_id={"tx": moved(1 << bit)}, device_id_type=pl.DeviceIdType.MESH
        )
    pl.semaphore_wait(barrier, steps)
    outs = (out_first, out_second)
    known = [[0], [0]]
    latest = [[], []]
    copies = []
    for step in range(steps):
        for stream in range(2):
            bit = orders[stream][steps - 1 - step]
            for copy in latest[stream]:
                copy.wait_recv()
            latest[stream] = []
            for mask in known[stream]:
                slot = mask | 1 << bit
                copy = pltpu.make_async_remote_copy(
                    src_ref=outs[stream].at[moved(mask)],
                    dst_ref=outs[stream].at[moved(mask)],
                    send_sem=send_sem.at[stream, slot],
                    recv_sem=recv_sem.at[stream, slot],
                    device_id={"tx": moved(1 << bit)},
                    device_id_type=pl.DeviceIdType.MESH,
                )
                copy.start()
                latest[stream].append(copy)
            copies += latest[stream]
            known[stream] = known[stream] + [mask | 1 << bit for mask in known[stream]]
    for stream in range(2):
        for copy in latest[stream]:
            copy.wait_recv()
    for copy in copies:
        copy.wait_send()


def gather_both(first, second):
    size = lax.axis_size("tx")
    rows, lanes = first.shape
    tall = -(-rows // 16) * 16
    whole = pl.BlockSpec(memory_space=pltpu.VMEM)
    outs = pl.pallas_call(
        functools.partial(doubling_kernel, size, bit_orders(size)),
        out_shape=[jax.ShapeDtypeStruct((size, tall, lanes), first.dtype)] * 2,
        in_specs=[whole] * 2,
        out_specs=[whole] * 2,
        scratch_shapes=[pltpu.SemaphoreType.DMA((2, size)), pltpu.SemaphoreType.DMA((2, size))],
        compiler_params=pltpu.CompilerParams(
            collective_id=1, has_side_effects=True, vmem_limit_bytes=16 * 1024 * 1024
        ),
    )(*(jnp.pad(x, ((0, tall - rows), (0, 0))) for x in (first, second)))
    return jnp.concatenate([x[:, :rows].reshape(-1, lanes) for x in outs], axis=1)


def reduce_both(first, second):
    size = lax.axis_size("tx")
    steps = size.bit_length() - 1
    rows = first.shape[0] // size
    tall = -(-rows // 16) * 16
    lanes = first.shape[1]
    first, second = (
        jnp.pad(x.reshape(size, rows, lanes), ((0, 0), (0, tall - rows), (0, 0)))
        for x in (first, second)
    )
    halves = [(size >> (step + 1), tall, lanes) for step in range(steps)] * 2
    whole = pl.BlockSpec(memory_space=pltpu.VMEM)
    outs = pl.pallas_call(
        functools.partial(halving_kernel, size, bit_orders(size)),
        out_shape=[jax.ShapeDtypeStruct((tall, lanes), jnp.float32)] * 2,
        in_specs=[whole] * 2,
        out_specs=[whole] * 2,
        scratch_shapes=[pltpu.VMEM(shape, jnp.bfloat16) for shape in halves * 2]
        + [pltpu.VMEM(shape, jnp.float32) for shape in halves]
        + [pltpu.SemaphoreType.DMA((2, steps)), pltpu.SemaphoreType.DMA((2, steps))],
        compiler_params=pltpu.CompilerParams(
            collective_id=0, has_side_effects=True, vmem_limit_bytes=32 * 1024 * 1024
        ),
    )(first, second)
    return [x[:rows] for x in outs]


CONTRACT = (((0,), (0,)), ((), ()))


def fill_windows(win, padded, lane, channels):
    for offset in range(27):
        a, b, c = (offset // 9, offset // 3 % 3, offset % 3)
        for i in range(BS):
            part = padded[a + i, b : b + BS, c : c + BS, :, lane : lane + channels]
            rows = BS * BS * SLOTS
            win[i * rows : (i + 1) * rows, offset * channels : (offset + 1) * channels] = (
                part.reshape(rows, channels)
            )


def row_tiles(win, body):
    rows = BS * BS * SLOTS

    def step(i, carry):
        body(pl.ds(pl.multiple_of(i * rows, rows), rows))
        return carry

    lax.fori_loop(0, win.shape[0] // rows, step, 0)


def kernel_gradient(win, cots, term):
    channels = term.shape[1]
    wide = 3 * channels

    def step(i, carry):
        columns = pl.ds(pl.multiple_of(i * wide, wide), wide)
        term[columns, :] = lax.dot_general(
            win[:, columns], cots[...], CONTRACT, preferred_element_type=jnp.float32
        )
        return carry

    lax.fori_loop(0, win.shape[1] // wide, step, 0)


def first_kernel(extended, choose, both_w, hidden, term, win, back, grad_mid, flipped, padded):
    channels = term.shape[1]
    fill_halo(padded, extended, choose)
    for offset in range(27):
        flipped[offset * channels : (offset + 1) * channels, :] = both_w[
            (26 - offset) * channels : (27 - offset) * channels, channels:
        ].T
    fill_windows(win, padded, channels, channels)

    def backward(rows):
        back[rows, :] = jnp.dot(win[rows, :], flipped[...], preferred_element_type=jnp.float32)

    row_tiles(win, backward)
    fill_windows(win, padded, 0, channels)

    def forward(rows):
        first_sum = jnp.dot(win[rows, :], both_w[:, :channels], preferred_element_type=jnp.float32)
        gate = jax.nn.sigmoid(first_sum)
        hidden[rows, :] = (first_sum * gate).astype(hidden.dtype)
        grad_mid[rows, :] = (
            back[rows, :] * gate * (1.0 + first_sum * (1.0 - gate))
        ).astype(grad_mid.dtype)

    row_tiles(win, forward)
    kernel_gradient(win, grad_mid, term)


def fill_halo(padded, extended, choose):
    wide = BS + 2
    brick, local = halo_tables(BS)
    for voxel in range(BS**3):
        places = [p for p in range(wide**3) if local[p] == voxel]
        rows = jnp.concatenate([choose[int(brick[p])] for p in places], axis=0)
        got = jnp.dot(rows, extended[voxel], preferred_element_type=jnp.float32)
        for k, p in enumerate(places):
            padded[p // (wide * wide), p // wide % wide, p % wide] = got[
                k * SLOTS : (k + 1) * SLOTS
            ].astype(padded.dtype)


def second_kernel(extended, cots, both_w, choose, out_map, term, win, padded):
    channels = term.shape[1]
    fill_halo(padded, extended, choose)
    fill_windows(win, padded, 0, channels)

    def forward(rows):
        out_map[rows, :] = jnp.dot(
            win[rows, :], both_w[:, channels:], preferred_element_type=jnp.float32
        ).astype(out_map.dtype)

    row_tiles(win, forward)
    kernel_gradient(win, cots, term)


def local_call(body, operands, extra):
    depth = operands[2].shape[0]
    channels = operands[2].shape[1] // 2
    rows = BS**3 * SLOTS
    whole = pl.BlockSpec(memory_space=pltpu.VMEM)
    return pl.pallas_call(
        body,
        out_shape=[
            jax.ShapeDtypeStruct((rows, channels), jnp.bfloat16),
            jax.ShapeDtypeStruct((depth, channels), jnp.float32),
        ],
        in_specs=[whole] * len(operands),
        out_specs=[whole] * 2,
        scratch_shapes=[pltpu.VMEM((rows, depth), jnp.bfloat16)]
        + [pltpu.VMEM(shape, kind) for shape, kind in extra],
        compiler_params=pltpu.CompilerParams(vmem_limit_bytes=40 * 1024 * 1024),
    )(*operands)


def on_device(features, nbr_table, rim_slots, w_first, w_second, cotangent):
    capacity, vox_count, channels = features.shape
    rim_count = rim_slots.shape[1] // 2
    chosen = rim_slots[0][:, None] == jnp.arange(capacity)[None, :]
    zero_slot = capacity + 2 * rim_count
    width = -(-(zero_slot + 1) // 16) * 16
    both_w = gather_both(w_first, w_second)

    table = jnp.pad(
        nbr_table, ((0, SLOTS - capacity), (0, 0)), constant_values=zero_slot
    ).T
    def extend(blocks):
        live = blocks[:, :capacity]
        packed = jnp.sum(
            jnp.where(chosen[None, :, :, None], live[:, None], 0), axis=2, dtype=jnp.float32
        ).astype(blocks.dtype)
        before, after = neighbours(packed, rim_count)
        extended = jnp.concatenate(
            [
                live,
                before,
                after,
                jnp.zeros((vox_count, width - zero_slot, blocks.shape[2]), blocks.dtype),
            ],
            axis=1,
        )
        return extended

    stacked = jnp.concatenate([features, cotangent], axis=2).transpose(1, 0, 2)
    wide = BS + 2
    choose = (table[:, :, None] == jnp.arange(width)).astype(jnp.bfloat16)
    rows = vox_count * SLOTS
    hidden, term_first = local_call(
        first_kernel,
        (extend(stacked), choose, both_w),
        (
            ((rows, channels), jnp.float32),
            ((rows, channels), jnp.bfloat16),
            ((both_w.shape[0], channels), jnp.bfloat16),
            ((wide, wide, wide, SLOTS, 2 * channels), jnp.bfloat16),
        ),
    )
    cot_rows = jnp.pad(
        stacked[..., channels:], ((0, 0), (0, SLOTS - capacity), (0, 0))
    ).reshape(-1, channels)
    out_map, term_second = local_call(
        second_kernel,
        (extend(hidden.reshape(vox_count, SLOTS, channels)), cot_rows, both_w, choose),
        (((wide, wide, wide, SLOTS, channels), jnp.bfloat16),),
    )
    out_map = out_map.reshape(vox_count, SLOTS, channels)[:, :capacity].transpose(1, 0, 2)
    grad_first, grad_second = reduce_both(term_first, term_second)
    return (out_map, grad_first, grad_second)


def solution(mesh):
    placed = (
        P(("groups", "tx"), None, None),
        P(("groups", "tx"), None),
        P(("groups", "tx"), None),
        P("tx", None),
        P("tx", None),
        P(("groups", "tx"), None, None),
    )
    return jax.shard_map(
        on_device,
        mesh=mesh,
        in_specs=placed,
        out_specs=(
            P(("groups", "tx"), None, None),
            P(("groups", "tx"), None),
            P(("groups", "tx"), None),
        ),
        check_vma=False,
    )
```

```python
import functools

import jax
import jax.numpy as jnp
import numpy as np
from jax import lax
from jax.experimental import pallas as pl
from jax.experimental.pallas import tpu as pltpu
from jax.sharding import PartitionSpec as P

BS = 4
SLOTS = 16


def halo_tables(side):
    wide = side + 2
    coords = np.arange(wide**3)
    brick = np.zeros(wide**3, np.int32)
    local = np.zeros(wide**3, np.int32)
    for along in (coords // (wide * wide), coords // wide % wide, coords % wide):
        moved = along - 1
        step = moved // side
        brick = brick * 3 + step + 1
        local = local * side + moved - step * side
    return (brick.astype(np.int32), local.astype(np.int32))


def neighbours(packed, rim_count):
    size = lax.axis_size("tx")
    up = [(i, (i + 1) % size) for i in range(size - 1)]
    down = [(j, i) for i, j in up]
    before = lax.ppermute(packed[:, rim_count:], "tx", up)
    after = lax.ppermute(packed[:, :rim_count], "tx", down)
    return (before, after)


def bit_orders(size):
    count = size.bit_length() - 1
    middle = 1 + (count - 1) // 2
    rest = list(range(middle, count)) + list(range(1, middle))
    return (list(range(count)), [0] + rest)


def halving_kernel(size, orders, first, second, out_first, out_second, *scratch):
    steps = size.bit_length() - 1
    sends, recvs, sums = (scratch[: 2 * steps], scratch[2 * steps : 4 * steps], scratch[4 * steps : -2])
    send_sem, recv_sem = scratch[-2:]
    me = lax.axis_index("tx")
    barrier = pltpu.get_barrier_semaphore()

    def bit_of(bit):
        return me // (1 << bit) % 2

    def partner(bit):
        return me + (1 - 2 * bit_of(bit)) * (1 << bit)

    for bit in range(steps):
        pl.semaphore_signal(
            barrier, inc=1, device_id={"tx": partner(bit)}, device_id_type=pl.DeviceIdType.MESH
        )
    pl.semaphore_wait(barrier, steps)

    held = [lambda i: first[i], lambda i: second[i]]
    left = [list(range(steps)), list(range(steps))]
    copies = [[], []]
    outs = (out_first, out_second)
    for step in range(steps + 1):
        for stream in range(2):
            if step:
                arrived = recvs[stream * steps + step - 1]
                copies[stream][-1].wait_recv()
                kept = keep[stream]

                def read(i, kept=kept, arrived=arrived):
                    return kept(i) + arrived[i].astype(jnp.float32)

            else:
                read = held[stream]
                if stream == 0:
                    keep = [None, None]
            if step == steps:
                outs[stream][...] = read(0)
                continue
            bit = orders[stream][step]
            low = 1 << left[stream].index(bit)
            left[stream].remove(bit)
            half = size >> (step + 1)
            mine = bit_of(bit)

            def entry(j, side, low=low):
                return j // low * (2 * low) + side * low + j % low

            out = sends[stream * steps + step]

            def pack(j, carry, out=out, read=read, entry=entry, mine=mine):
                out[j] = read(entry(j, 1 - mine)).astype(out.dtype)
                return carry

            lax.fori_loop(0, half, pack, 0)
            copy = pltpu.make_async_remote_copy(
                src_ref=out,
                dst_ref=recvs[stream * steps + step],
                send_sem=send_sem.at[stream, step],
                recv_sem=recv_sem.at[stream, step],
                device_id={"tx": partner(bit)},
                device_id_type=pl.DeviceIdType.MESH,
            )
            copy.start()
            copies[stream].append(copy)
            total = sums[stream * steps + step]

            def fold(j, carry, total=total, read=read, entry=entry, mine=mine):
                total[j] = read(entry(j, mine))
                return carry

            lax.fori_loop(0, half, fold, 0)
            keep[stream] = lambda i, total=total: total[i]
    for stream in range(2):
        for copy in copies[stream]:
            copy.wait_send()


def doubling_kernel(size, orders, first, second, out_first, out_second, send_sem, recv_sem):
    steps = size.bit_length() - 1
    me = lax.axis_index("tx")
    barrier = pltpu.get_barrier_semaphore()

    def moved(mask):
        place = me
        for bit in range(steps):
            if mask >> bit & 1:
                place = place + (1 - 2 * (me // (1 << bit) % 2)) * (1 << bit)
        return place

    out_first[me] = first[...]
    out_second[me] = second[...]
    for bit in range(steps):
        pl.semaphore_signal(
            barrier, inc=1, device_id={"tx": moved(1 << bit)}, device_id_type=pl.DeviceIdType.MESH
        )
    pl.semaphore_wait(barrier, steps)
    outs = (out_first, out_second)
    known = [[0], [0]]
    latest = [[], []]
    copies = []
    for step in range(steps):
        for stream in range(2):
            bit = orders[stream][steps - 1 - step]
            for copy in latest[stream]:
                copy.wait_recv()
            latest[stream] = []
            for mask in known[stream]:
                slot = mask | 1 << bit
                copy = pltpu.make_async_remote_copy(
                    src_ref=outs[stream].at[moved(mask)],
                    dst_ref=outs[stream].at[moved(mask)],
                    send_sem=send_sem.at[stream, slot],
                    recv_sem=recv_sem.at[stream, slot],
                    device_id={"tx": moved(1 << bit)},
                    device_id_type=pl.DeviceIdType.MESH,
                )
                copy.start()
                latest[stream].append(copy)
            copies += latest[stream]
            known[stream] = known[stream] + [mask | 1 << bit for mask in known[stream]]
    for stream in range(2):
        for copy in latest[stream]:
            copy.wait_recv()
    for copy in copies:
        copy.wait_send()


def gather_both(first, second):
    size = lax.axis_size("tx")
    rows, lanes = first.shape
    tall = -(-rows // 16) * 16
    whole = pl.BlockSpec(memory_space=pltpu.VMEM)
    outs = pl.pallas_call(
        functools.partial(doubling_kernel, size, bit_orders(size)),
        out_shape=[jax.ShapeDtypeStruct((size, tall, lanes), first.dtype)] * 2,
        in_specs=[whole] * 2,
        out_specs=[whole] * 2,
        scratch_shapes=[pltpu.SemaphoreType.DMA((2, size)), pltpu.SemaphoreType.DMA((2, size))],
        compiler_params=pltpu.CompilerParams(
            collective_id=1, has_side_effects=True, vmem_limit_bytes=16 * 1024 * 1024
        ),
    )(*(jnp.pad(x, ((0, tall - rows), (0, 0))) for x in (first, second)))
    return jnp.concatenate([x[:, :rows].reshape(-1, lanes) for x in outs], axis=1)


def reduce_both(first, second):
    size = lax.axis_size("tx")
    steps = size.bit_length() - 1
    rows = first.shape[0] // size
    tall = -(-rows // 16) * 16
    lanes = first.shape[1]
    first, second = (
        jnp.pad(x.reshape(size, rows, lanes), ((0, 0), (0, tall - rows), (0, 0)))
        for x in (first, second)
    )
    halves = [(size >> (step + 1), tall, lanes) for step in range(steps)] * 2
    whole = pl.BlockSpec(memory_space=pltpu.VMEM)
    outs = pl.pallas_call(
        functools.partial(halving_kernel, size, bit_orders(size)),
        out_shape=[jax.ShapeDtypeStruct((tall, lanes), jnp.float32)] * 2,
        in_specs=[whole] * 2,
        out_specs=[whole] * 2,
        scratch_shapes=[pltpu.VMEM(shape, jnp.bfloat16) for shape in halves * 2]
        + [pltpu.VMEM(shape, jnp.float32) for shape in halves]
        + [pltpu.SemaphoreType.DMA((2, steps)), pltpu.SemaphoreType.DMA((2, steps))],
        compiler_params=pltpu.CompilerParams(
            collective_id=0, has_side_effects=True, vmem_limit_bytes=32 * 1024 * 1024
        ),
    )(first, second)
    return [x[:rows] for x in outs]


CONTRACT = (((0,), (0,)), ((), ()))


def fill_windows(win, padded, lane, channels):
    for offset in range(27):
        a, b, c = (offset // 9, offset // 3 % 3, offset % 3)
        for i in range(BS):
            part = padded[a + i, b : b + BS, c : c + BS, :, lane : lane + channels]
            rows = BS * BS * SLOTS
            win[i * rows : (i + 1) * rows, offset * channels : (offset + 1) * channels] = (
                part.reshape(rows, channels)
            )


def row_tiles(win, body):
    rows = BS * BS * SLOTS

    def step(i, carry):
        body(pl.ds(pl.multiple_of(i * rows, rows), rows))
        return carry

    lax.fori_loop(0, win.shape[0] // rows, step, 0)


def kernel_gradient(win, cots, term):
    channels = term.shape[1]
    wide = 9 * channels

    def step(i, carry):
        columns = pl.ds(pl.multiple_of(i * wide, wide), wide)
        term[columns, :] = lax.dot_general(
            win[:, columns], cots[...], CONTRACT, preferred_element_type=jnp.float32
        )
        return carry

    lax.fori_loop(0, win.shape[1] // wide, step, 0)


def first_kernel(extended, choose, both_w, hidden, term, win, back, grad_mid, flipped, padded):
    channels = term.shape[1]
    fill_halo(padded, extended, choose)
    for offset in range(27):
        flipped[offset * channels : (offset + 1) * channels, :] = both_w[
            (26 - offset) * channels : (27 - offset) * channels, channels:
        ].T
    fill_windows(win, padded, channels, channels)

    def backward(rows):
        back[rows, :] = jnp.dot(win[rows, :], flipped[...], preferred_element_type=jnp.float32)

    row_tiles(win, backward)
    fill_windows(win, padded, 0, channels)

    def forward(rows):
        first_sum = jnp.dot(win[rows, :], both_w[:, :channels], preferred_element_type=jnp.float32)
        gate = jax.nn.sigmoid(first_sum)
        hidden[rows, :] = (first_sum * gate).astype(hidden.dtype)
        grad_mid[rows, :] = (
            back[rows, :] * gate * (1.0 + first_sum * (1.0 - gate))
        ).astype(grad_mid.dtype)

    row_tiles(win, forward)
    kernel_gradient(win, grad_mid, term)


def fill_halo(padded, extended, choose):
    wide = BS + 2
    brick, local = halo_tables(BS)
    for voxel in range(BS**3):
        places = [p for p in range(wide**3) if local[p] == voxel]
        rows = jnp.concatenate([choose[int(brick[p])] for p in places], axis=0)
        got = jnp.dot(rows, extended[voxel], preferred_element_type=jnp.float32)
        for k, p in enumerate(places):
            padded[p // (wide * wide), p // wide % wide, p % wide] = got[
                k * SLOTS : (k + 1) * SLOTS
            ].astype(padded.dtype)


def second_kernel(extended, cots, both_w, choose, out_map, term, win, padded):
    channels = term.shape[1]
    fill_halo(padded, extended, choose)
    fill_windows(win, padded, 0, channels)

    def forward(rows):
        out_map[rows, :] = jnp.dot(
            win[rows, :], both_w[:, channels:], preferred_element_type=jnp.float32
        ).astype(out_map.dtype)

    row_tiles(win, forward)
    kernel_gradient(win, cots, term)


def local_call(body, operands, extra):
    depth = operands[2].shape[0]
    channels = operands[2].shape[1] // 2
    rows = BS**3 * SLOTS
    whole = pl.BlockSpec(memory_space=pltpu.VMEM)
    return pl.pallas_call(
        body,
        out_shape=[
            jax.ShapeDtypeStruct((rows, channels), jnp.bfloat16),
            jax.ShapeDtypeStruct((depth, channels), jnp.float32),
        ],
        in_specs=[whole] * len(operands),
        out_specs=[whole] * 2,
        scratch_shapes=[pltpu.VMEM((rows, depth), jnp.bfloat16)]
        + [pltpu.VMEM(shape, kind) for shape, kind in extra],
        compiler_params=pltpu.CompilerParams(vmem_limit_bytes=40 * 1024 * 1024),
    )(*operands)


def on_device(features, nbr_table, rim_slots, w_first, w_second, cotangent):
    capacity, vox_count, channels = features.shape
    rim_count = rim_slots.shape[1] // 2
    chosen = rim_slots[0][:, None] == jnp.arange(capacity)[None, :]
    zero_slot = capacity + 2 * rim_count
    width = -(-(zero_slot + 1) // 16) * 16
    both_w = gather_both(w_first, w_second)

    table = jnp.pad(
        nbr_table, ((0, SLOTS - capacity), (0, 0)), constant_values=zero_slot
    ).T
    def extend(blocks):
        live = blocks[:, :capacity]
        packed = jnp.sum(
            jnp.where(chosen[None, :, :, None], live[:, None], 0), axis=2, dtype=jnp.float32
        ).astype(blocks.dtype)
        before, after = neighbours(packed, rim_count)
        extended = jnp.concatenate(
            [
                live,
                before,
                after,
                jnp.zeros((vox_count, width - zero_slot, blocks.shape[2]), blocks.dtype),
            ],
            axis=1,
        )
        return extended

    stacked = jnp.concatenate([features, cotangent], axis=2).transpose(1, 0, 2)
    wide = BS + 2
    choose = (table[:, :, None] == jnp.arange(width)).astype(jnp.bfloat16)
    rows = vox_count * SLOTS
    hidden, term_first = local_call(
        first_kernel,
        (extend(stacked), choose, both_w),
        (
            ((rows, channels), jnp.float32),
            ((rows, channels), jnp.bfloat16),
            ((both_w.shape[0], channels), jnp.bfloat16),
            ((wide, wide, wide, SLOTS, 2 * channels), jnp.bfloat16),
        ),
    )
    cot_rows = jnp.pad(
        stacked[..., channels:], ((0, 0), (0, SLOTS - capacity), (0, 0))
    ).reshape(-1, channels)
    out_map, term_second = local_call(
        second_kernel,
        (extend(hidden.reshape(vox_count, SLOTS, channels)), cot_rows, both_w, choose),
        (((wide, wide, wide, SLOTS, channels), jnp.bfloat16),),
    )
    out_map = out_map.reshape(vox_count, SLOTS, channels)[:, :capacity].transpose(1, 0, 2)
    grad_first, grad_second = reduce_both(term_first, term_second)
    return (out_map, grad_first, grad_second)


def solution(mesh):
    placed = (
        P(("groups", "tx"), None, None),
        P(("groups", "tx"), None),
        P(("groups", "tx"), None),
        P("tx", None),
        P("tx", None),
        P(("groups", "tx"), None, None),
    )
    return jax.shard_map(
        on_device,
        mesh=mesh,
        in_specs=placed,
        out_specs=(
            P(("groups", "tx"), None, None),
            P(("groups", "tx"), None),
            P(("groups", "tx"), None),
        ),
        check_vma=False,
    )
```
